32 devices in a mesh: expert: 8 (over y, x, core), tensor: 4 (over z).
Axes of the slice: x: 2, y: 2, z: 4, core: 2. Of those that a mesh axis runs over, the one named last changes fastest.
Arguments:
- picked_rows: bfloat16 [8, 256, 6144], P('expert', None, 'tensor'), may hold values from -6 to 6
- w_gate: bfloat16 [8, 6144, 1536], P('expert', 'tensor'), may hold values from -0.078125 to 0.078125
- w_up: bfloat16 [8, 6144, 1536], P('expert', 'tensor'), may hold values from -0.078125 to 0.078125
- w_down: bfloat16 [8, 1536, 6144], P('expert', None, 'tensor'), may hold values from -0.15625 to 0.15625
- combine_gate: float32 [8, 256], P('expert'), may hold values from 0.3 to 3
- pick_owner: int32 [8, 256], replicated, may hold values from 0 to 7, as said below
- pick_row: int32 [8, 256], replicated, may hold values from 0 to 191, as said below
- residual_in: bfloat16 [1536, 6144], P('expert', 'tensor'), may hold values from -60 to 60
- norm_gain: float32 [6144], P('tensor'), may hold values from 0.5 to 2
- projection: bfloat16 [6144, 6144], P('expert', 'tensor'), may hold values from -0.078125 to 0.078125
Outputs:
- projected: bfloat16 [1536, 6144], P('expert', 'tensor')
The draws below stay inside these ranges and needn't reach their ends.
Inputs may be any that keep to these rules, and one draw needn't show every extreme that they name: `pick_owner`: for every expert, at most 96 of its picks have one owner group, and one owner group gets exactly 96 picks from every expert. The picks of one expert are distinct tokens. `pick_row`: together with pick_owner it names a token; no expert names a token twice.
All inputs are finite; a program needn't handle non-finite values.
Results may differ from the reference program's by a relative error of at most 0.0051.
Values may be sent and summed in bfloat16 or wider, within the bound.
A program may use at most 64 MiB of HBM per device.

```python
import math
import jax
import jax.numpy as jnp
from jax import lax

D = 6144
FF = 1536
CAP = 256
EXPERTS = 8
TOK_GROUP = 192
TOKENS = 1536
MOST = 96
QKV = 6144


def choose_picks(key):
    hot_key, expert_keys = jax.random.split(key)
    hot_owner = jax.random.randint(hot_key, (), 0, EXPERTS)
    slot_owner = jnp.arange(EXPERTS * MOST, dtype=jnp.int32) // MOST

    def one_expert(expert_key):
        cand_key, score_key = jax.random.split(expert_key)
        owner_keys = jax.random.split(cand_key, EXPERTS)
        candidates = jax.vmap(lambda owner_key: jax.random.permutation(owner_key, TOK_GROUP)[:MOST])(owner_keys)
        rank_order = jax.random.permutation(score_key, EXPERTS * MOST)
        scores = rank_order + jnp.where(slot_owner == hot_owner, EXPERTS * MOST, 0)
        scores_top, chosen = lax.top_k(scores, CAP)
        return (slot_owner[chosen], candidates.reshape(-1)[chosen])
    owners, rows_all = jax.vmap(one_expert)(jax.random.split(expert_keys, EXPERTS))
    return (owners.astype(jnp.int32), rows_all.astype(jnp.int32))


def draw_pick_owner(key, part):
    owners, rows_all = choose_picks(key)
    return owners


def draw_pick_row(key, part):
    owners, rows_all = choose_picks(key)
    return rows_all


def draw_residual_in(key, part):
    key = jax.random.fold_in(key, 7)
    base_key, row_key, col_key = jax.random.split(key, 3)
    col_ramp = 3.0 ** (jnp.arange(D, dtype=jnp.float32) / D - 0.5)
    row_scale = jnp.exp(jax.random.uniform(row_key, (TOKENS, 1), jnp.float32, -1.15, 1.15))
    col_scale = jnp.exp(jax.random.uniform(col_key, (1, D), jnp.float32, -0.6, 0.6)) * col_ramp[None, :]
    values_base = jnp.clip(jax.random.normal(base_key, (TOKENS, D), jnp.float32), -4.0, 4.0)
    values = jnp.clip(values_base * row_scale * col_scale, -60.0, 60.0)
    return values.astype(jnp.bfloat16)


def levels(rng, dims, cuts, low, largest):
    factor_of = 1.0
    for position, shards_of in cuts:
        steps = jax.random.uniform(jax.random.fold_in(jax.random.fold_in(rng, 6), position), (shards_of,), jnp.float32, low / len(cuts), largest / len(cuts))
        factor_of = factor_of * jnp.repeat(jnp.exp(steps), dims[position] // shards_of).reshape((-1,) + (1,) * (len(dims) - 1 - position))
    return factor_of


def noise(rng, extent, scale, most, pieces=(), kind=jnp.bfloat16):
    drawn = jax.random.normal(rng, extent, jnp.float32) * scale
    if len(pieces) > 0:
        drawn = levels(rng, extent, pieces, -0.22, 0.18) * drawn
    return jnp.clip(drawn, min=-most, max=most).astype(kind)


def setup_inputs(seed: int = 0) -> dict:
    key_of = jax.random.split(jax.random.key(seed), 11)
    picked_rows = noise(key_of[0], (EXPERTS, CAP, D), 1.0, 6.0, ((0, 8), (2, 4)))
    w_gate = noise(key_of[1], (EXPERTS, D, FF), D ** -0.5, 0.078125, ((0, 8), (1, 4)))
    w_up = noise(key_of[2], (EXPERTS, D, FF), D ** -0.5, 0.078125, ((0, 8), (1, 4)))
    w_down = noise(key_of[3], (EXPERTS, FF, D), FF ** -0.5, 0.15625, ((0, 8), (2, 4)))
    combine_gate = jnp.clip(jnp.exp(math.log(3.0) - 2.3025851 * jax.random.uniform(key_of[4], (EXPERTS, CAP), jnp.float32) ** levels(key_of[4], (EXPERTS, CAP), ((0, 8),), -0.2, 0.2)), 0.3, 3.0)
    pick_owner = draw_pick_owner(jax.random.fold_in(key_of[10], 71), 0)
    pick_row = draw_pick_row(jax.random.fold_in(key_of[10], 71), 0)
    residual_in = draw_residual_in(jax.random.fold_in(key_of[10], 71), 0)
    norm_gain = jnp.clip(jnp.exp(math.log(2.0) - 1.3862944 * jax.random.uniform(key_of[8], (D,), jnp.float32) ** levels(key_of[8], (D,), ((0, 4),), -0.2, 0.2)), 0.5, 2.0)
    projection = noise(key_of[9], (D, QKV), D ** -0.5, 0.078125, ((0, 8), (1, 4)))
    return {"picked_rows": picked_rows, "w_gate": w_gate, "w_up": w_up, "w_down": w_down, "combine_gate": combine_gate, "pick_owner": pick_owner, "pick_row": pick_row, "residual_in": residual_in, "norm_gain": norm_gain, "projection": projection}


def expert_rows(operands):
    my_rows, gate_mat, up_mat, down_mat, weights = operands
    gate_pre = jnp.dot(my_rows, gate_mat, preferred_element_type=jnp.float32)
    up_pre = jnp.dot(my_rows, up_mat, preferred_element_type=jnp.float32)
    hidden = (jax.nn.silu(gate_pre) * up_pre).astype(jnp.bfloat16)
    output = jnp.dot(hidden, down_mat, preferred_element_type=jnp.float32)
    return (weights[:, None] * output).astype(jnp.bfloat16)

def reference(picked_rows, w_gate, w_up, w_down, combine_gate, pick_owner, pick_row, residual_in, norm_gain, projection):
    weighted = lax.map(expert_rows, (picked_rows, w_gate, w_up, w_down, combine_gate))
    target = (pick_owner * TOK_GROUP + pick_row).reshape(-1).astype(jnp.int32)
    moe = jnp.zeros((TOKENS, D), jnp.float32).at[target].add(weighted.reshape(-1, D).astype(jnp.float32))
    mixed = residual_in.astype(jnp.float32) + moe
    inverse_rms = lax.rsqrt(lax.optimization_barrier(jnp.mean(mixed * mixed, axis=1, keepdims=True)) + 1e-05)
    normed = (mixed * inverse_rms * norm_gain[None, :]).astype(jnp.bfloat16)
    return jnp.dot(normed, projection, preferred_element_type=jnp.float32).astype(jnp.bfloat16)
```

```python
import functools
import math

import jax
import jax.numpy as jnp
from jax import lax
from jax.experimental import pallas as pl
from jax.experimental.pallas import tpu as pltpu
from jax.sharding import PartitionSpec as P

MESH = pl.DeviceIdType.MESH
F32 = jnp.float32
BF16 = jnp.bfloat16
HI = lax.Precision.HIGHEST
HALVES = 2


def body(
    n, n_tensor, grid_a, grid_b, width,
    rows_hbm, gate_hbm, up_hbm, down_hbm, combine_ref, owner_ref, row_ref, resid_hbm, gain_ref, proj_hbm,
    out_ref,
    x, wg, wu, wd, resid, part, from_left, from_right, hid, cbuf, ebuf, proj, table, squares, acc,
    load_sem, rs_send, rs_recv, hid_send, hid_recv, c_send, c_recv, c_sib_send, c_sib_recv,
    e_send, e_recv, s_send, s_recv, p_send, p_recv, p_sib_send, p_sib_recv,
):
    e = lax.axis_index("expert")
    z = lax.axis_index("tensor")
    core = lax.rem(e, 2)
    chip = e // 2
    a, b = chip // grid_b, lax.rem(chip, grid_b)
    last = n_tensor - 1
    cap, d_z = x.shape
    ff = wg.shape[1]
    ff_half = ff // HALVES
    seg = cap // n_tensor
    chunks = d_z // width
    tokens = resid.shape[0]
    k_dev = proj_hbm.shape[0]
    k_half = k_dev // 2
    offsets = [(da, db) for da in range(grid_a) for db in range(grid_b)]

    def chip_at(da, db):
        return lax.rem(a + da + grid_a, grid_a) * grid_b + lax.rem(b + db + grid_b, grid_b)

    def to_expert(da, db):
        return {"expert": chip_at(da, db) * 2 + core}

    sibling = {"expert": chip * 2 + 1 - core}

    def remote(src, dst, send, recv, where):
        return pltpu.make_async_remote_copy(
            src_ref=src, dst_ref=dst, send_sem=send, recv_sem=recv, device_id=where, device_id_type=MESH
        )

    loads = [pltpu.make_async_copy(rows_hbm.at[0], x, load_sem.at[0])]
    for h in range(HALVES):
        cols = pl.ds(h * ff_half, ff_half)
        loads.append(pltpu.make_async_copy(gate_hbm.at[0, :, cols], wg.at[:, cols], load_sem.at[1 + 2 * h]))
        loads.append(pltpu.make_async_copy(up_hbm.at[0, :, cols], wu.at[:, cols], load_sem.at[2 + 2 * h]))
    base = 1 + 2 * HALVES
    loads.append(pltpu.make_async_copy(down_hbm.at[0], wd, load_sem.at[base]))
    loads.append(pltpu.make_async_copy(resid_hbm, resid, load_sem.at[base + 1]))
    my_k = pl.multiple_of(e * k_dev, 16)
    loads.append(pltpu.make_async_copy(proj_hbm, proj.at[pl.ds(my_k, k_dev)], load_sem.at[base + 2]))
    for load in loads:
        load.start()

    barrier = pltpu.get_barrier_semaphore()
    for i in range(1, n_tensor):
        pl.semaphore_signal(barrier, inc=1, device_id={"tensor": lax.rem(z + i, n_tensor)}, device_id_type=MESH)
    for da in range(1, grid_a):
        pl.semaphore_signal(barrier, inc=1, device_id=to_expert(da, 0), device_id_type=MESH)
    for db in range(1, grid_b):
        pl.semaphore_signal(barrier, inc=1, device_id=to_expert(0, db), device_id_type=MESH)
    pl.semaphore_signal(barrier, inc=1, device_id=sibling, device_id_type=MESH)
    pl.semaphore_wait(barrier, n_tensor - 1 + grid_a - 1 + grid_b - 1 + 1)

    sends = []

    def begin(copy):
        copy.start()
        sends.append(copy)

    def slot(da, db):
        return da * grid_b + db

    def proj_rows(da, db, k, half=None):
        start = (chip_at(-da, -db) * 2 + k) * k_dev
        if half is None:
            return proj.at[pl.ds(pl.multiple_of(start, 16), k_dev)]
        return proj.at[pl.ds(pl.multiple_of(start + half * k_half, 16), k_half)]

    mine = proj.at[pl.ds(my_k, k_dev)]
    for da, db in offsets[1:]:
        if da == 0 or db == 0:
            begin(remote(proj_hbm, mine, p_send.at[slot(da, db), 0], p_recv.at[slot(da, db), 0], to_expert(da, db)))
    begin(remote(proj_hbm, mine, p_sib_send.at[0], p_sib_recv.at[0], sibling))

    loads[0].wait()
    tile = 256
    for h in range(HALVES):
        loads[1 + 2 * h].wait()
        loads[2 + 2 * h].wait()

        @pl.loop(0, ff_half // tile)
        def _(j):
            src = pl.ds(pl.multiple_of(h * ff_half + j * tile, tile), tile)
            part[h, :, pl.ds(pl.multiple_of(j * tile, tile), tile)] = jnp.dot(
                x[...], wg[:, src], preferred_element_type=F32
            )
            part[h, :, pl.ds(pl.multiple_of(ff_half + j * tile, tile), tile)] = jnp.dot(
                x[...], wu[:, src], preferred_element_type=F32
            )

        @pl.when((z == 0) | (z == last))
        def _():
            for step in range(n_tensor - 1):
                rs_step(step, h, z, last, seg, part, from_left, from_right, rs_send, rs_recv, remote)

    def rs_middle(h):
        @pl.when((z > 0) & (z < last))
        def _():
            for step in range(n_tensor - 1):
                rs_step(step, h, z, last, seg, part, from_left, from_right, rs_send, rs_recv, remote)

    token = lax.broadcasted_iota(jnp.int32, (tokens, cap), 0)
    for da, db in offsets:
        for r in range(2):
            source = chip_at(-da, -db) * 2 + (core if r == 0 else 1 - core)
            owner = owner_ref[pl.ds(source, 1), :]
            row = row_ref[pl.ds(source, 1), :]
            target = jnp.where(owner == e, row, -1)
            table[slot(da, db), r] = jnp.where(target == token, 1.0, 0.0).astype(BF16)

    my_seg = pl.ds(pl.multiple_of(z * seg, seg), seg)
    def rs_final(h):
        @pl.when(z > 0)
        def _():
            remote(from_left.at[h, z], from_left.at[h, z], rs_send.at[0, h, z], rs_recv.at[0, h, z], {"tensor": z}).wait_recv()
            part[h, my_seg, :] += from_left[h, z].astype(F32)

        @pl.when(z < last)
        def _():
            remote(from_right.at[h, z], from_right.at[h, z], rs_send.at[1, h, z], rs_recv.at[1, h, z], {"tensor": z}).wait_recv()
            part[h, my_seg, :] += from_right[h, z].astype(F32)

        gate = part[h, my_seg, :ff_half]
        up = part[h, my_seg, ff_half:]
        hid[h, z] = (gate / (1.0 + jnp.exp(-gate)) * up).astype(BF16)
        chain_own(hid.at[h], hid_send.at[h], hid_recv.at[h], z, last, remote)

    for step in range(n_tensor + HALVES - 1):
        if step < HALVES:
            rs_middle(step)
        for h in range(HALVES):
            if 1 <= step - h < n_tensor:
                chain_pass(step - h, hid.at[h], hid_send.at[h], hid_recv.at[h], z, last, remote)
        if step < HALVES:
            rs_final(step)

    loads[base].wait()
    loads[base + 1].wait()
    weight = lax.dot_general(
        jnp.broadcast_to(combine_ref[...], (8, cap)), jnp.full((8, width), 0.125, F32),
        (((0,), (0,)), ((), ())), precision=HI, preferred_element_type=F32,
    )
    cap_half = cap // 2

    def c_block(q, da, db, r=0, half=None):
        ref = cbuf.at[q, slot(da, db), r]
        return ref if half is None else ref.at[pl.ds(half * cap_half, cap_half)]

    def stage_send(q):
        cols = pl.ds(q * width, width)
        total = 0.0
        for h in range(HALVES):
            total += jnp.dot(
                hid[h].reshape(cap, ff_half), wd[pl.ds(h * ff_half, ff_half), cols], preferred_element_type=F32
            )
        cbuf[q, 0, 0] = (weight * total).astype(BF16)
        own = c_block(q, 0, 0)
        for da, db in offsets[1:]:
            if da == 0 or db == 0:
                s = slot(da, db)
                begin(remote(own, c_block(q, da, db), c_send.at[q, s, 0, 0], c_recv.at[q, s, 0], to_expert(da, db)))
        begin(remote(own, c_block(q, 0, 0, 1), c_sib_send.at[q, 0], c_sib_recv.at[q, 0], sibling))

    def arrived(ref, send, recv):
        remote(ref, ref, send, recv, sibling).wait_recv()

    def stage_forward(q):
        for da, db in offsets[1:]:
            if da != 0 and db != 0:
                continue
            s = slot(da, db)
            block = c_block(q, da, db)
            arrived(block, c_send.at[q, s, 0, 0], c_recv.at[q, s, 0])
            if db == 0:
                for d in range(1, grid_b):
                    t = slot(da, d)
                    begin(remote(c_block(q, da, 0, 0, 0), c_block(q, da, d, 0, 0), c_send.at[q, t, 0, 0], c_recv.at[q, t, 0], to_expert(0, d)))
            else:
                for d in range(1, grid_a):
                    t = slot(d, db)
                    begin(remote(c_block(q, 0, db, 0, 1), c_block(q, d, db, 0, 1), c_send.at[q, t, 1, 0], c_recv.at[q, t, 1], to_expert(d, 0)))
            begin(remote(block, c_block(q, da, db, 1), c_sib_send.at[q, s], c_sib_recv.at[q, s], sibling))

    def stage_combine(q):
        for da, db in offsets:
            if da == 0 or db == 0:
                continue
            s = slot(da, db)
            for half in range(2):
                arrived(c_block(q, da, db, 0, half), c_send.at[q, s, half, 0], c_recv.at[q, s, half])
            block = c_block(q, da, db)
            begin(remote(block, c_block(q, da, db, 1), c_sib_send.at[q, s], c_sib_recv.at[q, s], sibling))
        cols = pl.ds(q * width, width)
        mixed = resid[:, cols].astype(F32)
        for da, db in offsets:
            s = slot(da, db)
            mixed += jnp.dot(table[s, 0], cbuf[q, s, 0], preferred_element_type=F32)
        for da, db in offsets:
            s = slot(da, db)
            arrived(c_block(q, da, db, 1), c_sib_send.at[q, s], c_sib_recv.at[q, s])
            mixed += jnp.dot(table[s, 1], cbuf[q, s, 1], preferred_element_type=F32)
        ebuf[q, z] = (mixed * gain_ref[:, cols]).astype(BF16)
        chain_own(ebuf.at[q], e_send.at[q], e_recv.at[q], z, last, remote)
        return lax.dot_general(
            jnp.ones((8, width), F32), mixed * mixed, (((1,), (1,)), ((), ())), precision=HI,
            preferred_element_type=F32,
        )

    square_sum = 0.0
    for t in range(chunks + 2):
        if t < chunks:
            stage_send(t)
        if 0 <= t - 1 < chunks:
            stage_forward(t - 1)
        if 0 <= t - 2 < chunks:
            square_sum += stage_combine(t - 2)
            for i in range(1, n_tensor):
                if t - 2 - i >= 0:
                    chain_pass(i, ebuf.at[t - 2 - i], e_send.at[t - 2 - i], e_recv.at[t - 2 - i], z, last, remote)
        if t == chunks:
            for da, db in offsets[1:]:
                if da != 0 and db != 0:
                    continue
                s = slot(da, db)
                block = proj_rows(da, db, core)
                arrived(block, p_send.at[s, 0], p_recv.at[s, 0])
                if db == 0:
                    for d in range(1, grid_b):
                        u = slot(da, d)
                        ref = proj_rows(da, 0, core, 0)
                        begin(remote(ref, ref, p_send.at[u, 0], p_recv.at[u, 0], to_expert(0, d)))
                else:
                    for d in range(1, grid_a):
                        u = slot(d, db)
                        ref = proj_rows(0, db, core, 1)
                        begin(remote(ref, ref, p_send.at[u, 1], p_recv.at[u, 1], to_expert(d, 0)))
                begin(remote(block, block, p_sib_send.at[s], p_sib_recv.at[s], sibling))

    squares[z] = square_sum
    for i in range(1, n_tensor):
        begin(remote(squares.at[z], squares.at[z], s_send.at[i], s_recv.at[i], {"tensor": lax.rem(z + i, n_tensor)}))
    for step in range(chunks - n_tensor, chunks + n_tensor):
        for i in range(1, n_tensor):
            q = step - i
            if 0 <= q < chunks and q + i > chunks - 1:
                chain_pass(i, ebuf.at[q], e_send.at[q], e_recv.at[q], z, last, remote)

    total_squares = squares[z]
    for i in range(1, n_tensor):
        origin = lax.rem(z + n_tensor - i, n_tensor)
        remote(squares.at[origin], squares.at[origin], s_send.at[i], s_recv.at[i], {"tensor": z}).wait_recv()
        total_squares += squares[origin]
    col = 512 if d_z % 512 == 0 else 128
    column_total = lax.dot_general(
        total_squares, jnp.full((8, col), 0.125, F32), (((0,), (0,)), ((), ())), precision=HI,
        preferred_element_type=F32,
    )
    inverse_rms = lax.rsqrt(column_total / (d_z * n_tensor) + 1e-05)

    loads[base + 2].wait()
    order = [o for o in offsets if o[0] == 0 or o[1] == 0] + [o for o in offsets if o[0] != 0 and o[1] != 0]
    for da, db in order:
        if da != 0 and db != 0:
            s = slot(da, db)
            for half in range(2):
                arrived(proj_rows(da, db, core, half), p_send.at[s, half], p_recv.at[s, half])
            block = proj_rows(da, db, core)
            begin(remote(block, block, p_sib_send.at[s], p_sib_recv.at[s], sibling))
    for pos, (da, db) in enumerate(order):
        s = slot(da, db)
        arrived(proj_rows(da, db, 1 - core), p_sib_send.at[s], p_sib_recv.at[s])
        source = chip_at(-da, -db)

        @pl.loop(0, d_z // col)
        def _(j):
            cols = pl.ds(pl.multiple_of(j * col, col), col)
            total = 0.0 if pos == 0 else acc[:, cols]
            for q in range(chunks):
                k = pl.ds(pl.multiple_of(source * 2 * k_dev + q * width, 128), width)
                total += jnp.dot(ebuf[q, source], proj[k, cols], preferred_element_type=F32)
            if pos == len(order) - 1:
                out_ref[:, cols] = (total * inverse_rms).astype(BF16)
            else:
                acc[:, cols] = total

    for copy in sends:
        copy.wait_send()
    for h in range(HALVES):
        for step in range(n_tensor - 1):
            right, left = n_tensor - 1 - step, step

            @pl.when(z < right)
            def _():
                remote(from_left.at[h, right], from_left.at[h, right], rs_send.at[0, h, right], rs_recv.at[0, h, right], {"tensor": z + 1}).wait_send()

            @pl.when(z > left)
            def _():
                remote(from_right.at[h, left], from_right.at[h, left], rs_send.at[1, h, left], rs_recv.at[1, h, left], {"tensor": z - 1}).wait_send()
        chain_end(hid.at[h], hid_send.at[h], hid_recv.at[h], z, last, remote)
    for q in range(chunks):
        chain_end(ebuf.at[q], e_send.at[q], e_recv.at[q], z, last, remote)


def rs_step(step, h, z, last, seg, part, from_left, from_right, send, recv, remote):
    right, left = last - step, step

    def go_right():
        @pl.when(z < right)
        def _():
            block = part[h, pl.ds(right * seg, seg), :]
            slot = from_left.at[h, right]
            copy = remote(slot, slot, send.at[0, h, right], recv.at[0, h, right], {"tensor": z + 1})

            @pl.when(z > 0)
            def _():
                copy.wait_recv()
                from_left[h, right] = (from_left[h, right].astype(F32) + block).astype(BF16)

            @pl.when(z == 0)
            def _():
                from_left[h, right] = block.astype(BF16)

            copy.start()

    def go_left():
        @pl.when(z > left)
        def _():
            block = part[h, pl.ds(left * seg, seg), :]
            slot = from_right.at[h, left]
            copy = remote(slot, slot, send.at[1, h, left], recv.at[1, h, left], {"tensor": z - 1})

            @pl.when(z < last)
            def _():
                copy.wait_recv()
                from_right[h, left] = (from_right[h, left].astype(F32) + block).astype(BF16)

            @pl.when(z == last)
            def _():
                from_right[h, left] = block.astype(BF16)

            copy.start()

    @pl.when(2 * z < last)
    def _():
        go_right()
        go_left()

    @pl.when(2 * z >= last)
    def _():
        go_left()
        go_right()


def chain_copy(buf, send, recv, origin, way, target, remote):
    return remote(buf.at[origin], buf.at[origin], send.at[way, origin], recv.at[way, origin], {"tensor": target})


def chain_own(buf, send, recv, z, last, remote):
    @pl.when(z < last)
    def _():
        chain_copy(buf, send, recv, z, 0, z + 1, remote).start()

    @pl.when(z > 0)
    def _():
        chain_copy(buf, send, recv, z, 1, z - 1, remote).start()


def chain_pass(i, buf, send, recv, z, last, remote):
    @pl.when(z >= i)
    def _():
        copy = chain_copy(buf, send, recv, z - i, 0, z + 1, remote)
        copy.wait_recv()

        @pl.when(z < last)
        def _():
            copy.start()

    @pl.when(z + i <= last)
    def _():
        copy = chain_copy(buf, send, recv, z + i, 1, z - 1, remote)
        copy.wait_recv()

        @pl.when(z > 0)
        def _():
            copy.start()


def chain_end(buf, send, recv, z, last, remote):
    for origin in range(last + 1):
        @pl.when((z >= origin) & (z < last))
        def _():
            chain_copy(buf, send, recv, origin, 0, z + 1, remote).wait_send()

        @pl.when((z <= origin) & (z > 0))
        def _():
            chain_copy(buf, send, recv, origin, 1, z - 1, remote).wait_send()


def solution(mesh):
    n, n_tensor = mesh.shape["expert"], mesh.shape["tensor"]
    chips = n // 2
    grid_b = math.isqrt(chips)
    grid_a = chips // grid_b
    assert grid_a * grid_b == chips and chips == n_tensor

    def shards(picked_rows, w_gate, w_up, w_down, combine_gate, pick_owner, pick_row, residual_in, norm_gain, projection):
        _, cap, d_z = picked_rows.shape
        ff = w_gate.shape[2]
        tokens = residual_in.shape[0]
        k_dev = projection.shape[0]
        width = 384
        chunks = d_z // width
        seg = cap // n_tensor
        hbm = pl.BlockSpec(memory_space=pl.ANY)
        vmem = pl.BlockSpec(memory_space=pltpu.VMEM)
        dma = pltpu.SemaphoreType.DMA
        return pl.pallas_call(
            functools.partial(body, n, n_tensor, grid_a, grid_b, width),
            out_shape=jax.ShapeDtypeStruct((tokens, d_z), BF16),
            in_specs=[hbm, hbm, hbm, hbm, vmem, vmem, vmem, hbm, vmem, hbm],
            out_specs=vmem,
            scratch_shapes=[
                pltpu.VMEM((cap, d_z), BF16),
                pltpu.VMEM((d_z, ff), BF16),
                pltpu.VMEM((d_z, ff), BF16),
                pltpu.VMEM((ff, d_z), BF16),
                pltpu.VMEM((tokens, d_z), BF16),
                pltpu.VMEM((HALVES, cap, 2 * ff // HALVES), F32),
                pltpu.VMEM((HALVES, n_tensor, seg, 2 * ff // HALVES), BF16),
                pltpu.VMEM((HALVES, n_tensor, seg, 2 * ff // HALVES), BF16),
                pltpu.VMEM((HALVES, n_tensor, seg, ff // HALVES), BF16),
                pltpu.VMEM((chunks, chips, 2, cap, width), BF16),
                pltpu.VMEM((chunks, n_tensor, tokens, width), BF16),
                pltpu.VMEM((n * k_dev, d_z), BF16),
                pltpu.VMEM((chips, 2, tokens, cap), BF16),
                pltpu.VMEM((n_tensor, 8, tokens), F32),
                pltpu.VMEM((tokens, d_z), F32),
                dma((4 + 2 * HALVES,)),
                dma((2, HALVES, n_tensor)),
                dma((2, HALVES, n_tensor)),
                dma((HALVES, 2, n_tensor)),
                dma((HALVES, 2, n_tensor)),
                dma((chunks, chips, 2, 1)),
                dma((chunks, chips, 2)),
                dma((chunks, chips)),
                dma((chunks, chips)),
                dma((chunks, 2, n_tensor)),
                dma((chunks, 2, n_tensor)),
                dma((n_tensor,)),
                dma((n_tensor,)),
                dma((chips, 2)),
                dma((chips, 2)),
                dma((chips,)),
                dma((chips,)),
            ],
            compiler_params=pltpu.CompilerParams(
                collective_id=0, has_side_effects=True, vmem_limit_bytes=60 * 2**20
            ),
            name="layer",
        )(picked_rows, w_gate, w_up, w_down, combine_gate, pick_owner, pick_row, residual_in, norm_gain[None, :], projection)

    return jax.shard_map(
        shards,
        mesh=mesh,
        in_specs=(
            P("expert", None, "tensor"),
            P("expert", "tensor", None),
            P("expert", "tensor", None),
            P("expert", None, "tensor"),
            P("expert", None),
            P(),
            P(),
            P("expert", "tensor"),
            P("tensor"),
            P("expert", "tensor"),
        ),
        out_specs=P("expert", "tensor"),
        check_vma=False,
    )
```

```python
import functools
import math

import jax
import jax.numpy as jnp
from jax import lax
from jax.experimental import pallas as pl
from jax.experimental.pallas import tpu as pltpu
from jax.sharding import PartitionSpec as P

MESH = pl.DeviceIdType.MESH
F32 = jnp.float32
BF16 = jnp.bfloat16
HI = lax.Precision.HIGHEST
HALVES = 2
PIECES = 3


def body(
    n, n_tensor, grid_a, grid_b, width,
    rows_hbm, gate_hbm, up_hbm, down_hbm, combine_ref, owner_ref, row_ref, resid_hbm, gain_ref, proj_hbm,
    out_ref,
    x, wg, wu, wd, resid, part, from_left, from_right, hid, cbuf, ebuf, proj, table, squares, acc,
    load_sem, rs_send, rs_recv, hid_send, hid_recv, c_send, c_recv, c_sib_send, c_sib_recv,
    e_send, e_recv, s_send, s_recv, p_send, p_recv, p_sib_send, p_sib_recv,
):
    e = lax.axis_index("expert")
    z = lax.axis_index("tensor")
    core = lax.rem(e, 2)
    chip = e // 2
    a, b = chip // grid_b, lax.rem(chip, grid_b)
    last = n_tensor - 1
    cap, d_z = x.shape
    ff = wg.shape[1]
    ff_half = ff // HALVES
    seg = cap // n_tensor
    chunks = d_z // width
    tokens = resid.shape[0]
    k_dev = proj_hbm.shape[0]
    k_half = k_dev // 2
    k_piece = k_half // PIECES
    offsets = [(da, db) for da in range(grid_a) for db in range(grid_b)]

    def chip_at(da, db):
        return lax.rem(a + da + grid_a, grid_a) * grid_b + lax.rem(b + db + grid_b, grid_b)

    def to_expert(da, db):
        return {"expert": chip_at(da, db) * 2 + core}

    sibling = {"expert": chip * 2 + 1 - core}

    def remote(src, dst, send, recv, where):
        return pltpu.make_async_remote_copy(
            src_ref=src, dst_ref=dst, send_sem=send, recv_sem=recv, device_id=where, device_id_type=MESH
        )

    loads = [pltpu.make_async_copy(rows_hbm.at[0], x, load_sem.at[0])]
    for h in range(HALVES):
        cols = pl.ds(h * ff_half, ff_half)
        loads.append(pltpu.make_async_copy(gate_hbm.at[0, :, cols], wg.at[:, cols], load_sem.at[1 + 2 * h]))
        loads.append(pltpu.make_async_copy(up_hbm.at[0, :, cols], wu.at[:, cols], load_sem.at[2 + 2 * h]))
    base = 1 + 2 * HALVES
    loads.append(pltpu.make_async_copy(down_hbm.at[0], wd, load_sem.at[base]))
    loads.append(pltpu.make_async_copy(resid_hbm, resid, load_sem.at[base + 1]))
    my_k = pl.multiple_of(e * k_dev, 16)
    loads.append(pltpu.make_async_copy(proj_hbm, proj.at[pl.ds(my_k, k_dev)], load_sem.at[base + 2]))
    for load in loads:
        load.start()

    barrier = pltpu.get_barrier_semaphore()
    for i in range(1, n_tensor):
        pl.semaphore_signal(barrier, inc=1, device_id={"tensor": lax.rem(z + i, n_tensor)}, device_id_type=MESH)
    for da in range(1, grid_a):
        pl.semaphore_signal(barrier, inc=1, device_id=to_expert(da, 0), device_id_type=MESH)
    for db in range(1, grid_b):
        pl.semaphore_signal(barrier, inc=1, device_id=to_expert(0, db), device_id_type=MESH)
    pl.semaphore_signal(barrier, inc=1, device_id=sibling, device_id_type=MESH)
    pl.semaphore_wait(barrier, n_tensor - 1 + grid_a - 1 + grid_b - 1 + 1)

    sends = []

    def begin(copy):
        copy.start()
        sends.append(copy)

    def slot(da, db):
        return da * grid_b + db

    def proj_rows(da, db, k, half=None, piece=0):
        start = (chip_at(-da, -db) * 2 + k) * k_dev
        if half is None:
            return proj.at[pl.ds(pl.multiple_of(start, 16), k_dev)]
        return proj.at[pl.ds(pl.multiple_of(start + half * k_half + piece * k_piece, 16), k_piece)]

    mine = proj.at[pl.ds(my_k, k_dev)]
    for da, db in offsets[1:]:
        if da == 0 or db == 0:
            begin(remote(proj_hbm, mine, p_send.at[slot(da, db), 0], p_recv.at[slot(da, db), 0], to_expert(da, db)))
    begin(remote(proj_hbm, mine, p_sib_send.at[0, 0], p_sib_recv.at[0, 0], sibling))

    loads[0].wait()
    tile = 256
    for h in range(HALVES):
        loads[1 + 2 * h].wait()
        loads[2 + 2 * h].wait()

        @pl.loop(0, ff_half // tile)
        def _(j):
            src = pl.ds(pl.multiple_of(h * ff_half + j * tile, tile), tile)
            part[h, :, pl.ds(pl.multiple_of(j * tile, tile), tile)] = jnp.dot(
                x[...], wg[:, src], preferred_element_type=F32
            )
            part[h, :, pl.ds(pl.multiple_of(ff_half + j * tile, tile), tile)] = jnp.dot(
                x[...], wu[:, src], preferred_element_type=F32
            )

        @pl.when((z == 0) | (z == last))
        def _():
            for step in range(n_tensor - 1):
                rs_step(step, h, z, last, seg, part, from_left, from_right, rs_send, rs_recv, remote)

    def rs_middle(h):
        @pl.when((z > 0) & (z < last))
        def _():
            for step in range(n_tensor - 1):
                rs_step(step, h, z, last, seg, part, from_left, from_right, rs_send, rs_recv, remote)

    token = lax.broadcasted_iota(jnp.int32, (tokens, cap), 0)
    for da, db in offsets:
        for r in range(2):
            source = chip_at(-da, -db) * 2 + (core if r == 0 else 1 - core)
            owner = owner_ref[pl.ds(source, 1), :]
            row = row_ref[pl.ds(source, 1), :]
            target = jnp.where(owner == e, row, -1)
            table[slot(da, db), r] = jnp.where(target == token, 1.0, 0.0).astype(BF16)

    my_seg = pl.ds(pl.multiple_of(z * seg, seg), seg)
    def rs_final(h):
        @pl.when(z > 0)
        def _():
            remote(from_left.at[h, z], from_left.at[h, z], rs_send.at[0, h, z], rs_recv.at[0, h, z], {"tensor": z}).wait_recv()
            part[h, my_seg, :] += from_left[h, z].astype(F32)

        @pl.when(z < last)
        def _():
            remote(from_right.at[h, z], from_right.at[h, z], rs_send.at[1, h, z], rs_recv.at[1, h, z], {"tensor": z}).wait_recv()
            part[h, my_seg, :] += from_right[h, z].astype(F32)

        gate = part[h, my_seg, :ff_half]
        up = part[h, my_seg, ff_half:]
        hid[h, z] = (gate / (1.0 + jnp.exp(-gate)) * up).astype(BF16)
        chain_own(hid.at[h], hid_send.at[h], hid_recv.at[h], z, last, remote)

    for step in range(n_tensor + HALVES - 1):
        if step < HALVES:
            rs_middle(step)
        for h in range(HALVES):
            if 1 <= step - h < n_tensor:
                chain_pass(step - h, hid.at[h], hid_send.at[h], hid_recv.at[h], z, last, remote)
        if step < HALVES:
            rs_final(step)

    loads[base].wait()
    loads[base + 1].wait()
    weight = lax.dot_general(
        jnp.broadcast_to(combine_ref[...], (8, cap)), jnp.full((8, width), 0.125, F32),
        (((0,), (0,)), ((), ())), precision=HI, preferred_element_type=F32,
    )
    cap_half = cap // 2

    def c_block(q, da, db, r=0, half=None):
        ref = cbuf.at[q, slot(da, db), r]
        return ref if half is None else ref.at[pl.ds(half * cap_half, cap_half)]

    def stage_send(q):
        cols = pl.ds(q * width, width)
        total = 0.0
        for h in range(HALVES):
            total += jnp.dot(
                hid[h].reshape(cap, ff_half), wd[pl.ds(h * ff_half, ff_half), cols], preferred_element_type=F32
            )
        cbuf[q, 0, 0] = (weight * total).astype(BF16)
        own = c_block(q, 0, 0)
        for da, db in offsets[1:]:
            if da == 0 or db == 0:
                s = slot(da, db)
                begin(remote(own, c_block(q, da, db), c_send.at[q, s, 0, 0], c_recv.at[q, s, 0], to_expert(da, db)))
        begin(remote(own, c_block(q, 0, 0, 1), c_sib_send.at[q, 0], c_sib_recv.at[q, 0], sibling))

    def arrived(ref, send, recv):
        remote(ref, ref, send, recv, sibling).wait_recv()

    def stage_forward(q):
        for da, db in offsets[1:]:
            if da != 0 and db != 0:
                continue
            s = slot(da, db)
            block = c_block(q, da, db)
            arrived(block, c_send.at[q, s, 0, 0], c_recv.at[q, s, 0])
            if db == 0:
                for d in range(1, grid_b):
                    t = slot(da, d)
                    begin(remote(c_block(q, da, 0, 0, 0), c_block(q, da, d, 0, 0), c_send.at[q, t, 0, 0], c_recv.at[q, t, 0], to_expert(0, d)))
            else:
                for d in range(1, grid_a):
                    t = slot(d, db)
                    begin(remote(c_block(q, 0, db, 0, 1), c_block(q, d, db, 0, 1), c_send.at[q, t, 1, 0], c_recv.at[q, t, 1], to_expert(d, 0)))
            begin(remote(block, c_block(q, da, db, 1), c_sib_send.at[q, s], c_sib_recv.at[q, s], sibling))

    def stage_combine(q):
        for da, db in offsets:
            if da == 0 or db == 0:
                continue
            s = slot(da, db)
            for half in range(2):
                arrived(c_block(q, da, db, 0, half), c_send.at[q, s, half, 0], c_recv.at[q, s, half])
            block = c_block(q, da, db)
            begin(remote(block, c_block(q, da, db, 1), c_sib_send.at[q, s], c_sib_recv.at[q, s], sibling))
        cols = pl.ds(q * width, width)
        mixed = resid[:, cols].astype(F32)
        for da, db in offsets:
            s = slot(da, db)
            mixed += jnp.dot(table[s, 0], cbuf[q, s, 0], preferred_element_type=F32)
        for da, db in offsets:
            s = slot(da, db)
            arrived(c_block(q, da, db, 1), c_sib_send.at[q, s], c_sib_recv.at[q, s])
            mixed += jnp.dot(table[s, 1], cbuf[q, s, 1], preferred_element_type=F32)
        ebuf[q, z] = (mixed * gain_ref[cols].reshape(1, width)).astype(BF16)
        chain_own(ebuf.at[q], e_send.at[q], e_recv.at[q], z, last, remote)
        return lax.dot_general(
            jnp.ones((8, width), F32), mixed * mixed, (((1,), (1,)), ((), ())), precision=HI,
            preferred_element_type=F32,
        )

    square_sum = 0.0
    for t in range(chunks + 2):
        if t < chunks:
            stage_send(t)
        if 0 <= t - 1 < chunks:
            stage_forward(t - 1)
        if t == chunks:
            for da, db in offsets[1:]:
                if da != 0 and db != 0:
                    continue
                s = slot(da, db)
                block = proj_rows(da, db, core)
                arrived(block, p_send.at[s, 0], p_recv.at[s, 0])
                if db == 0:
                    for d in range(1, grid_b):
                        u = slot(da, d)
                        for piece in range(PIECES):
                            ref = proj_rows(da, 0, core, 0, piece)
                            begin(remote(ref, ref, p_send.at[u, piece], p_recv.at[u, piece], to_expert(0, d)))
                else:
                    for d in range(1, grid_a):
                        u = slot(d, db)
                        for piece in range(PIECES):
                            ref = proj_rows(0, db, core, 1, piece)
                            p = PIECES + piece
                            begin(remote(ref, ref, p_send.at[u, p], p_recv.at[u, p], to_expert(d, 0)))
                begin(remote(block, block, p_sib_send.at[s, 0], p_sib_recv.at[s, 0], sibling))
        if 0 <= t - 2 < chunks:
            square_sum += stage_combine(t - 2)
            for i in range(1, n_tensor):
                if t - 2 - i >= 0:
                    chain_pass(i, ebuf.at[t - 2 - i], e_send.at[t - 2 - i], e_recv.at[t - 2 - i], z, last, remote)

    squares[z] = square_sum
    for i in range(1, n_tensor):
        begin(remote(squares.at[z], squares.at[z], s_send.at[i], s_recv.at[i], {"tensor": lax.rem(z + i, n_tensor)}))
    for step in range(chunks - n_tensor, chunks + n_tensor):
        for i in range(1, n_tensor):
            q = step - i
            if 0 <= q < chunks and q + i > chunks - 1:
                chain_pass(i, ebuf.at[q], e_send.at[q], e_recv.at[q], z, last, remote)

    total_squares = squares[z]
    for i in range(1, n_tensor):
        origin = lax.rem(z + n_tensor - i, n_tensor)
        remote(squares.at[origin], squares.at[origin], s_send.at[i], s_recv.at[i], {"tensor": z}).wait_recv()
        total_squares += squares[origin]
    col = 512 if d_z % 512 == 0 else 128
    column_total = lax.dot_general(
        total_squares, jnp.full((8, col), 0.125, F32), (((0,), (0,)), ((), ())), precision=HI,
        preferred_element_type=F32,
    )
    inverse_rms = lax.rsqrt(column_total / (d_z * n_tensor) + 1e-05)

    loads[base + 2].wait()
    near = [o for o in offsets if o[0] == 0 or o[1] == 0]
    far = [o for o in offsets if o[0] != 0 and o[1] != 0]
    order = near + far

    def hand_over(piece):
        for da, db in far:
            s = slot(da, db)
            for half in range(2):
                p = half * PIECES + piece
                block = proj_rows(da, db, core, half, piece)
                arrived(block, p_send.at[s, p], p_recv.at[s, p])
                begin(remote(block, block, p_sib_send.at[s, p], p_sib_recv.at[s, p], sibling))

    assert len(near) >= PIECES
    for pos, (da, db) in enumerate(order):
        s = slot(da, db)
        if pos < len(near):
            arrived(proj_rows(da, db, 1 - core), p_sib_send.at[s, 0], p_sib_recv.at[s, 0])
        else:
            for half in range(2):
                for piece in range(PIECES):
                    p = half * PIECES + piece
                    arrived(proj_rows(da, db, 1 - core, half, piece), p_sib_send.at[s, p], p_sib_recv.at[s, p])
        source = chip_at(-da, -db)

        @pl.loop(0, d_z // col)
        def _(j):
            cols = pl.ds(pl.multiple_of(j * col, col), col)
            total = 0.0 if pos == 0 else acc[:, cols]
            for q in range(chunks):
                k = pl.ds(pl.multiple_of(source * 2 * k_dev + q * width, 128), width)
                total += jnp.dot(ebuf[q, source], proj[k, cols], preferred_element_type=F32)
            if pos == len(order) - 1:
                out_ref[:, cols] = (total * inverse_rms).astype(BF16)
            else:
                acc[:, cols] = total

        if pos < PIECES:
            hand_over(pos)

    for copy in sends:
        copy.wait_send()
    for h in range(HALVES):
        for step in range(n_tensor - 1):
            right, left = n_tensor - 1 - step, step

            @pl.when(z < right)
            def _():
                remote(from_left.at[h, right], from_left.at[h, right], rs_send.at[0, h, right], rs_recv.at[0, h, right], {"tensor": z + 1}).wait_send()

            @pl.when(z > left)
            def _():
                remote(from_right.at[h, left], from_right.at[h, left], rs_send.at[1, h, left], rs_recv.at[1, h, left], {"tensor": z - 1}).wait_send()
        chain_end(hid.at[h], hid_send.at[h], hid_recv.at[h], z, last, remote)
    for q in range(chunks):
        chain_end(ebuf.at[q], e_send.at[q], e_recv.at[q], z, last, remote)


def rs_step(step, h, z, last, seg, part, from_left, from_right, send, recv, remote):
    right, left = last - step, step

    def go_right():
        @pl.when(z < right)
        def _():
            block = part[h, pl.ds(right * seg, seg), :]
            slot = from_left.at[h, right]
            copy = remote(slot, slot, send.at[0, h, right], recv.at[0, h, right], {"tensor": z + 1})

            @pl.when(z > 0)
            def _():
                copy.wait_recv()
                from_left[h, right] = (from_left[h, right].astype(F32) + block).astype(BF16)

            @pl.when(z == 0)
            def _():
                from_left[h, right] = block.astype(BF16)

            copy.start()

    def go_left():
        @pl.when(z > left)
        def _():
            block = part[h, pl.ds(left * seg, seg), :]
            slot = from_right.at[h, left]
            copy = remote(slot, slot, send.at[1, h, left], recv.at[1, h, left], {"tensor": z - 1})

            @pl.when(z < last)
            def _():
                copy.wait_recv()
                from_right[h, left] = (from_right[h, left].astype(F32) + block).astype(BF16)

            @pl.when(z == last)
            def _():
                from_right[h, left] = block.astype(BF16)

            copy.start()

    @pl.when(2 * z < last)
    def _():
        go_right()
        go_left()

    @pl.when(2 * z >= last)
    def _():
        go_left()
        go_right()


def chain_copy(buf, send, recv, origin, way, target, remote):
    return remote(buf.at[origin], buf.at[origin], send.at[way, origin], recv.at[way, origin], {"tensor": target})


def chain_own(buf, send, recv, z, last, remote):
    @pl.when(z < last)
    def _():
        chain_copy(buf, send, recv, z, 0, z + 1, remote).start()

    @pl.when(z > 0)
    def _():
        chain_copy(buf, send, recv, z, 1, z - 1, remote).start()


def chain_pass(i, buf, send, recv, z, last, remote):
    @pl.when(z >= i)
    def _():
        copy = chain_copy(buf, send, recv, z - i, 0, z + 1, remote)
        copy.wait_recv()

        @pl.when(z < last)
        def _():
            copy.start()

    @pl.when(z + i <= last)
    def _():
        copy = chain_copy(buf, send, recv, z + i, 1, z - 1, remote)
        copy.wait_recv()

        @pl.when(z > 0)
        def _():
            copy.start()


def chain_end(buf, send, recv, z, last, remote):
    for origin in range(last + 1):
        @pl.when((z >= origin) & (z < last))
        def _():
            chain_copy(buf, send, recv, origin, 0, z + 1, remote).wait_send()

        @pl.when((z <= origin) & (z > 0))
        def _():
            chain_copy(buf, send, recv, origin, 1, z - 1, remote).wait_send()


def solution(mesh):
    n, n_tensor = mesh.shape["expert"], mesh.shape["tensor"]
    chips = n // 2
    grid_b = math.isqrt(chips)
    grid_a = chips // grid_b
    assert grid_a * grid_b == chips and chips == n_tensor

    def shards(picked_rows, w_gate, w_up, w_down, combine_gate, pick_owner, pick_row, residual_in, norm_gain, projection):
        _, cap, d_z = picked_rows.shape
        ff = w_gate.shape[2]
        tokens = residual_in.shape[0]
        k_dev = projection.shape[0]
        width = 384
        chunks = d_z // width
        seg = cap // n_tensor
        hbm = pl.BlockSpec(memory_space=pl.ANY)
        vmem = pl.BlockSpec(memory_space=pltpu.VMEM)
        dma = pltpu.SemaphoreType.DMA
        return pl.pallas_call(
            functools.partial(body, n, n_tensor, grid_a, grid_b, width),
            out_shape=jax.ShapeDtypeStruct((tokens, d_z), BF16),
            in_specs=[hbm, hbm, hbm, hbm, vmem, vmem, vmem, hbm, vmem, hbm],
            out_specs=vmem,
            scratch_shapes=[
                pltpu.VMEM((cap, d_z), BF16),
                pltpu.VMEM((d_z, ff), BF16),
                pltpu.VMEM((d_z, ff), BF16),
                pltpu.VMEM((ff, d_z), BF16),
                pltpu.VMEM((tokens, d_z), BF16),
                pltpu.VMEM((HALVES, cap, 2 * ff // HALVES), F32),
                pltpu.VMEM((HALVES, n_tensor, seg, 2 * ff // HALVES), BF16),
                pltpu.VMEM((HALVES, n_tensor, seg, 2 * ff // HALVES), BF16),
                pltpu.VMEM((HALVES, n_tensor, seg, ff // HALVES), BF16),
                pltpu.VMEM((chunks, chips, 2, cap, width), BF16),
                pltpu.VMEM((chunks, n_tensor, tokens, width), BF16),
                pltpu.VMEM((n * k_dev, d_z), BF16),
                pltpu.VMEM((chips, 2, tokens, cap), BF16),
                pltpu.VMEM((n_tensor, 8, tokens), F32),
                pltpu.VMEM((tokens, d_z), F32),
                dma((4 + 2 * HALVES,)),
                dma((2, HALVES, n_tensor)),
                dma((2, HALVES, n_tensor)),
                dma((HALVES, 2, n_tensor)),
                dma((HALVES, 2, n_tensor)),
                dma((chunks, chips, 2, 1)),
                dma((chunks, chips, 2)),
                dma((chunks, chips)),
                dma((chunks, chips)),
                dma((chunks, 2, n_tensor)),
                dma((chunks, 2, n_tensor)),
                dma((n_tensor,)),
                dma((n_tensor,)),
                dma((chips, 2 * PIECES)),
                dma((chips, 2 * PIECES)),
                dma((chips, 2 * PIECES)),
                dma((chips, 2 * PIECES)),
            ],
            compiler_params=pltpu.CompilerParams(
                collective_id=0, has_side_effects=True, vmem_limit_bytes=60 * 2**20
            ),
            name="layer",
        )(picked_rows, w_gate, w_up, w_down, combine_gate, pick_owner, pick_row, residual_in, norm_gain, projection)

    return jax.shard_map(
        shards,
        mesh=mesh,
        in_specs=(
            P("expert", None, "tensor"),
            P("expert", "tensor", None),
            P("expert", "tensor", None),
            P("expert", None, "tensor"),
            P("expert", None),
            P(),
            P(),
            P("expert", "tensor"),
            P("tensor"),
            P("expert", "tensor"),
        ),
        out_specs=P("expert", "tensor"),
        check_vma=False,
    )
```

```python
import functools
import math

import jax
import jax.numpy as jnp
from jax import lax
from jax.experimental import pallas as pl
from jax.experimental.pallas import tpu as pltpu
from jax.sharding import PartitionSpec as P

MESH = pl.DeviceIdType.MESH
F32 = jnp.float32
BF16 = jnp.bfloat16
HI = lax.Precision.HIGHEST
HALVES = 2
PIECES = 3


def body(
    n, n_tensor, grid_a, grid_b, width,
    rows_hbm, gate_hbm, up_hbm, down_hbm, combine_ref, owner_ref, row_ref, resid_hbm, gain_ref, proj_hbm,
    out_ref,
    x, wg, wu, wd, resid, part, from_left, from_right, hid, cbuf, ebuf, proj, table, squares, acc,
    load_sem, rs_send, rs_recv, hid_send, hid_recv, c_send, c_recv, c_sib_send, c_sib_recv,
    e_send, e_recv, s_send, s_recv, p_send, p_recv, p_sib_send, p_sib_recv,
):
    e = lax.axis_index("expert")
    z = lax.axis_index("tensor")
    core = lax.rem(e, 2)
    chip = e // 2
    a, b = chip // grid_b, lax.rem(chip, grid_b)
    last = n_tensor - 1
    cap, d_z = x.shape
    ff = wg.shape[1]
    ff_half = ff // HALVES
    seg = cap // n_tensor
    chunks = d_z // width
    tokens = resid.shape[0]
    k_dev = proj_hbm.shape[0]
    k_half = k_dev // 2
    k_piece = k_half // PIECES
    offsets = [(da, db) for da in range(grid_a) for db in range(grid_b)]

    def chip_at(da, db):
        return lax.rem(a + da + grid_a, grid_a) * grid_b + lax.rem(b + db + grid_b, grid_b)

    def to_expert(da, db):
        return {"expert": chip_at(da, db) * 2 + core}

    sibling = {"expert": chip * 2 + 1 - core}

    def remote(src, dst, send, recv, where):
        return pltpu.make_async_remote_copy(
            src_ref=src, dst_ref=dst, send_sem=send, recv_sem=recv, device_id=where, device_id_type=MESH
        )

    loads = [pltpu.make_async_copy(rows_hbm.at[0], x, load_sem.at[0])]
    for h in range(HALVES):
        cols = pl.ds(h * ff_half, ff_half)
        loads.append(pltpu.make_async_copy(gate_hbm.at[0, :, cols], wg.at[:, cols], load_sem.at[1 + 2 * h]))
        loads.append(pltpu.make_async_copy(up_hbm.at[0, :, cols], wu.at[:, cols], load_sem.at[2 + 2 * h]))
    base = 1 + 2 * HALVES
    loads.append(pltpu.make_async_copy(down_hbm.at[0], wd, load_sem.at[base]))
    loads.append(pltpu.make_async_copy(resid_hbm, resid, load_sem.at[base + 1]))
    my_k = pl.multiple_of(e * k_dev, 16)
    loads.append(pltpu.make_async_copy(proj_hbm, proj.at[pl.ds(my_k, k_dev)], load_sem.at[base + 2]))
    for load in loads:
        load.start()

    barrier = pltpu.get_barrier_semaphore()
    for i in range(1, n_tensor):
        pl.semaphore_signal(barrier, inc=1, device_id={"tensor": lax.rem(z + i, n_tensor)}, device_id_type=MESH)
    for da in range(1, grid_a):
        pl.semaphore_signal(barrier, inc=1, device_id=to_expert(da, 0), device_id_type=MESH)
    for db in range(1, grid_b):
        pl.semaphore_signal(barrier, inc=1, device_id=to_expert(0, db), device_id_type=MESH)
    pl.semaphore_signal(barrier, inc=1, device_id=sibling, device_id_type=MESH)
    pl.semaphore_wait(barrier, n_tensor - 1 + grid_a - 1 + grid_b - 1 + 1)

    sends = []

    def begin(copy):
        copy.start()
        sends.append(copy)

    def slot(da, db):
        return da * grid_b + db

    def proj_rows(da, db, k, half=None, piece=0):
        start = (chip_at(-da, -db) * 2 + k) * k_dev
        if half is None:
            return proj.at[pl.ds(pl.multiple_of(start, 16), k_dev)]
        return proj.at[pl.ds(pl.multiple_of(start + half * k_half + piece * k_piece, 16), k_piece)]

    near = [o for o in offsets[1:] if o[0] == 0 or o[1] == 0]
    far = [o for o in offsets if o[0] != 0 and o[1] != 0]

    def near_span(da, late):
        early = k_dev - k_piece
        if da != 0:
            return (early, k_piece) if late else (0, early)
        return (0, k_piece) if late else (k_piece, early)

    def near_rows(da, db, k, late):
        start, size = near_span(da, late)
        start += (chip_at(-da, -db) * 2 + k) * k_dev
        return proj.at[pl.ds(pl.multiple_of(start, 16), size)]

    def near_send(late):
        for da, db in near:
            start, size = near_span(da, late)
            s = slot(da, db)
            src = proj_hbm.at[pl.ds(start, size)]
            dst = proj.at[pl.ds(pl.multiple_of(my_k + start, 16), size)]
            begin(remote(src, dst, p_send.at[s, late], p_recv.at[s, late], to_expert(da, db)))

    mine = proj.at[pl.ds(my_k, k_dev)]
    near_send(0)
    begin(remote(proj_hbm, mine, p_sib_send.at[0, 0], p_sib_recv.at[0, 0], sibling))

    loads[0].wait()
    tile = 256
    for h in range(HALVES):
        loads[1 + 2 * h].wait()
        loads[2 + 2 * h].wait()

        @pl.loop(0, ff_half // tile)
        def _(j):
            src = pl.ds(pl.multiple_of(h * ff_half + j * tile, tile), tile)
            part[h, :, pl.ds(pl.multiple_of(j * tile, tile), tile)] = jnp.dot(
                x[...], wg[:, src], preferred_element_type=F32
            )
            part[h, :, pl.ds(pl.multiple_of(ff_half + j * tile, tile), tile)] = jnp.dot(
                x[...], wu[:, src], preferred_element_type=F32
            )

        @pl.when((z == 0) | (z == last))
        def _():
            for step in range(n_tensor - 1):
                rs_step(step, h, z, last, seg, part, from_left, from_right, rs_send, rs_recv, remote)

    def rs_middle(h):
        @pl.when((z > 0) & (z < last))
        def _():
            for step in range(n_tensor - 1):
                rs_step(step, h, z, last, seg, part, from_left, from_right, rs_send, rs_recv, remote)

    token = lax.broadcasted_iota(jnp.int32, (tokens, cap), 0)
    for da, db in offsets:
        for r in range(2):
            source = chip_at(-da, -db) * 2 + (core if r == 0 else 1 - core)
            owner = owner_ref[pl.ds(source, 1), :]
            row = row_ref[pl.ds(source, 1), :]
            target = jnp.where(owner == e, row, -1)
            table[slot(da, db), r] = jnp.where(target == token, 1.0, 0.0).astype(BF16)

    my_seg = pl.ds(pl.multiple_of(z * seg, seg), seg)
    def rs_final(h):
        @pl.when(z > 0)
        def _():
            remote(from_left.at[h, z], from_left.at[h, z], rs_send.at[0, h, z], rs_recv.at[0, h, z], {"tensor": z}).wait_recv()
            part[h, my_seg, :] += from_left[h, z].astype(F32)

        @pl.when(z < last)
        def _():
            remote(from_right.at[h, z], from_right.at[h, z], rs_send.at[1, h, z], rs_recv.at[1, h, z], {"tensor": z}).wait_recv()
            part[h, my_seg, :] += from_right[h, z].astype(F32)

        gate = part[h, my_seg, :ff_half]
        up = part[h, my_seg, ff_half:]
        hid[h, z] = (gate / (1.0 + jnp.exp(-gate)) * up).astype(BF16)
        chain_own(hid.at[h], hid_send.at[h], hid_recv.at[h], z, last, remote)

    for step in range(n_tensor + HALVES - 1):
        if step < HALVES:
            rs_middle(step)
        for h in range(HALVES):
            if 1 <= step - h < n_tensor:
                chain_pass(step - h, hid.at[h], hid_send.at[h], hid_recv.at[h], z, last, remote)
        if step < HALVES:
            rs_final(step)

    loads[base].wait()
    loads[base + 1].wait()
    weight = lax.dot_general(
        jnp.broadcast_to(combine_ref[...], (8, cap)), jnp.full((8, width), 0.125, F32),
        (((0,), (0,)), ((), ())), precision=HI, preferred_element_type=F32,
    )
    cap_half = cap // 2

    def c_block(q, da, db, r=0, half=None):
        ref = cbuf.at[q, slot(da, db), r]
        return ref if half is None else ref.at[pl.ds(half * cap_half, cap_half)]

    def stage_send(q):
        cols = pl.ds(q * width, width)
        total = 0.0
        for h in range(HALVES):
            total += jnp.dot(
                hid[h].reshape(cap, ff_half), wd[pl.ds(h * ff_half, ff_half), cols], preferred_element_type=F32
            )
        cbuf[q, 0, 0] = (weight * total).astype(BF16)
        own = c_block(q, 0, 0)
        for da, db in offsets[1:]:
            if da == 0 or db == 0:
                s = slot(da, db)
                begin(remote(own, c_block(q, da, db), c_send.at[q, s, 0, 0], c_recv.at[q, s, 0], to_expert(da, db)))
        begin(remote(own, c_block(q, 0, 0, 1), c_sib_send.at[q, 0], c_sib_recv.at[q, 0], sibling))

    def arrived(ref, send, recv):
        remote(ref, ref, send, recv, sibling).wait_recv()

    def stage_forward(q):
        for da, db in offsets[1:]:
            if da != 0 and db != 0:
                continue
            s = slot(da, db)
            block = c_block(q, da, db)
            arrived(block, c_send.at[q, s, 0, 0], c_recv.at[q, s, 0])
            if db == 0:
                for d in range(1, grid_b):
                    t = slot(da, d)
                    begin(remote(c_block(q, da, 0, 0, 0), c_block(q, da, d, 0, 0), c_send.at[q, t, 0, 0], c_recv.at[q, t, 0], to_expert(0, d)))
            else:
                for d in range(1, grid_a):
                    t = slot(d, db)
                    begin(remote(c_block(q, 0, db, 0, 1), c_block(q, d, db, 0, 1), c_send.at[q, t, 1, 0], c_recv.at[q, t, 1], to_expert(d, 0)))
            begin(remote(block, c_block(q, da, db, 1), c_sib_send.at[q, s], c_sib_recv.at[q, s], sibling))

    def stage_combine(q):
        for da, db in offsets:
            if da == 0 or db == 0:
                continue
            s = slot(da, db)
            for half in range(2):
                arrived(c_block(q, da, db, 0, half), c_send.at[q, s, half, 0], c_recv.at[q, s, half])
            block = c_block(q, da, db)
            begin(remote(block, c_block(q, da, db, 1), c_sib_send.at[q, s], c_sib_recv.at[q, s], sibling))
        cols = pl.ds(q * width, width)
        mixed = resid[:, cols].astype(F32)
        for da, db in offsets:
            s = slot(da, db)
            mixed += jnp.dot(table[s, 0], cbuf[q, s, 0], preferred_element_type=F32)
        for da, db in offsets:
            s = slot(da, db)
            arrived(c_block(q, da, db, 1), c_sib_send.at[q, s], c_sib_recv.at[q, s])
            mixed += jnp.dot(table[s, 1], cbuf[q, s, 1], preferred_element_type=F32)
        ebuf[q, z] = (mixed * gain_ref[cols].reshape(1, width)).astype(BF16)
        chain_own(ebuf.at[q], e_send.at[q], e_recv.at[q], z, last, remote)
        return lax.dot_general(
            jnp.ones((8, width), F32), mixed * mixed, (((1,), (1,)), ((), ())), precision=HI,
            preferred_element_type=F32,
        )

    square_sum = 0.0
    for t in range(chunks + 2):
        if t < chunks:
            stage_send(t)
        if 0 <= t - 1 < chunks:
            stage_forward(t - 1)
        if 0 <= t - 2 < chunks:
            square_sum += stage_combine(t - 2)
            for i in range(1, n_tensor):
                if t - 2 - i >= 0:
                    chain_pass(i, ebuf.at[t - 2 - i], e_send.at[t - 2 - i], e_recv.at[t - 2 - i], z, last, remote)
        if t == chunks:
            near_send(1)
            for da, db in near:
                block = near_rows(da, db, core, 0)
                arrived(block, p_send.at[slot(da, db), 0], p_recv.at[slot(da, db), 0])
                if db == 0:
                    for d in range(1, grid_b):
                        u = slot(da, d)
                        for piece in range(PIECES):
                            ref = proj_rows(da, 0, core, 0, piece)
                            begin(remote(ref, ref, p_send.at[u, piece], p_recv.at[u, piece], to_expert(0, d)))
                else:
                    for d in range(1, grid_a):
                        u = slot(d, db)
                        for piece in range(PIECES):
                            ref = proj_rows(0, db, core, 1, piece)
                            p = PIECES + piece
                            begin(remote(ref, ref, p_send.at[u, p], p_recv.at[u, p], to_expert(d, 0)))

    for da, db in near:
        block = near_rows(da, db, core, 0)
        begin(remote(block, block, p_sib_send.at[slot(da, db), 0], p_sib_recv.at[slot(da, db), 0], sibling))

    squares[z] = square_sum
    for i in range(1, n_tensor):
        begin(remote(squares.at[z], squares.at[z], s_send.at[i], s_recv.at[i], {"tensor": lax.rem(z + i, n_tensor)}))
    for step in range(chunks - n_tensor, chunks + n_tensor):
        for i in range(1, n_tensor):
            q = step - i
            if 0 <= q < chunks and q + i > chunks - 1:
                chain_pass(i, ebuf.at[q], e_send.at[q], e_recv.at[q], z, last, remote)

    total_squares = squares[z]
    for i in range(1, n_tensor):
        origin = lax.rem(z + n_tensor - i, n_tensor)
        remote(squares.at[origin], squares.at[origin], s_send.at[i], s_recv.at[i], {"tensor": z}).wait_recv()
        total_squares += squares[origin]
    col = 512 if d_z % 512 == 0 else 128
    column_total = lax.dot_general(
        total_squares, jnp.full((8, col), 0.125, F32), (((0,), (0,)), ((), ())), precision=HI,
        preferred_element_type=F32,
    )
    inverse_rms = lax.rsqrt(column_total / (d_z * n_tensor) + 1e-05)

    loads[base + 2].wait()
    order = [(0, 0)] + near + far

    def hand_over_late():
        for da, db in near:
            s = slot(da, db)
            block = near_rows(da, db, core, 1)
            arrived(block, p_send.at[s, 1], p_recv.at[s, 1])
            begin(remote(block, block, p_sib_send.at[s, 1], p_sib_recv.at[s, 1], sibling))

    def hand_over(piece):
        for da, db in far:
            s = slot(da, db)
            for half in range(2):
                p = half * PIECES + piece
                block = proj_rows(da, db, core, half, piece)
                arrived(block, p_send.at[s, p], p_recv.at[s, p])
                begin(remote(block, block, p_sib_send.at[s, p], p_sib_recv.at[s, p], sibling))

    assert len(near) + 1 >= PIECES
    for pos, (da, db) in enumerate(order):
        s = slot(da, db)
        if pos == 0:
            arrived(proj_rows(da, db, 1 - core), p_sib_send.at[s, 0], p_sib_recv.at[s, 0])
        elif pos <= len(near):
            for late in range(2):
                arrived(near_rows(da, db, 1 - core, late), p_sib_send.at[s, late], p_sib_recv.at[s, late])
        else:
            for half in range(2):
                for piece in range(PIECES):
                    p = half * PIECES + piece
                    arrived(proj_rows(da, db, 1 - core, half, piece), p_sib_send.at[s, p], p_sib_recv.at[s, p])
        source = chip_at(-da, -db)

        @pl.loop(0, d_z // col)
        def _(j):
            cols = pl.ds(pl.multiple_of(j * col, col), col)
            total = 0.0 if pos == 0 else acc[:, cols]
            for q in range(chunks):
                k = pl.ds(pl.multiple_of(source * 2 * k_dev + q * width, 128), width)
                total += jnp.dot(ebuf[q, source], proj[k, cols], preferred_element_type=F32)
            if pos == len(order) - 1:
                out_ref[:, cols] = (total * inverse_rms).astype(BF16)
            else:
                acc[:, cols] = total

        if pos == 0:
            hand_over_late()
        if pos < PIECES:
            hand_over(pos)

    for copy in sends:
        copy.wait_send()
    for h in range(HALVES):
        for step in range(n_tensor - 1):
            right, left = n_tensor - 1 - step, step

            @pl.when(z < right)
            def _():
                remote(from_left.at[h, right], from_left.at[h, right], rs_send.at[0, h, right], rs_recv.at[0, h, right], {"tensor": z + 1}).wait_send()

            @pl.when(z > left)
            def _():
                remote(from_right.at[h, left], from_right.at[h, left], rs_send.at[1, h, left], rs_recv.at[1, h, left], {"tensor": z - 1}).wait_send()
        chain_end(hid.at[h], hid_send.at[h], hid_recv.at[h], z, last, remote)
    for q in range(chunks):
        chain_end(ebuf.at[q], e_send.at[q], e_recv.at[q], z, last, remote)


def rs_step(step, h, z, last, seg, part, from_left, from_right, send, recv, remote):
    right, left = last - step, step

    def go_right():
        @pl.when(z < right)
        def _():
            block = part[h, pl.ds(right * seg, seg), :]
            slot = from_left.at[h, right]
            copy = remote(slot, slot, send.at[0, h, right], recv.at[0, h, right], {"tensor": z + 1})

            @pl.when(z > 0)
            def _():
                copy.wait_recv()
                from_left[h, right] = (from_left[h, right].astype(F32) + block).astype(BF16)

            @pl.when(z == 0)
            def _():
                from_left[h, right] = block.astype(BF16)

            copy.start()

    def go_left():
        @pl.when(z > left)
        def _():
            block = part[h, pl.ds(left * seg, seg), :]
            slot = from_right.at[h, left]
            copy = remote(slot, slot, send.at[1, h, left], recv.at[1, h, left], {"tensor": z - 1})

            @pl.when(z < last)
            def _():
                copy.wait_recv()
                from_right[h, left] = (from_right[h, left].astype(F32) + block).astype(BF16)

            @pl.when(z == last)
            def _():
                from_right[h, left] = block.astype(BF16)

            copy.start()

    @pl.when(2 * z < last)
    def _():
        go_right()
        go_left()

    @pl.when(2 * z >= last)
    def _():
        go_left()
        go_right()


def chain_copy(buf, send, recv, origin, way, target, remote):
    return remote(buf.at[origin], buf.at[origin], send.at[way, origin], recv.at[way, origin], {"tensor": target})


def chain_own(buf, send, recv, z, last, remote):
    @pl.when(z < last)
    def _():
        chain_copy(buf, send, recv, z, 0, z + 1, remote).start()

    @pl.when(z > 0)
    def _():
        chain_copy(buf, send, recv, z, 1, z - 1, remote).start()


def chain_pass(i, buf, send, recv, z, last, remote):
    @pl.when(z >= i)
    def _():
        copy = chain_copy(buf, send, recv, z - i, 0, z + 1, remote)
        copy.wait_recv()

        @pl.when(z < last)
        def _():
            copy.start()

    @pl.when(z + i <= last)
    def _():
        copy = chain_copy(buf, send, recv, z + i, 1, z - 1, remote)
        copy.wait_recv()

        @pl.when(z > 0)
        def _():
            copy.start()


def chain_end(buf, send, recv, z, last, remote):
    for origin in range(last + 1):
        @pl.when((z >= origin) & (z < last))
        def _():
            chain_copy(buf, send, recv, origin, 0, z + 1, remote).wait_send()

        @pl.when((z <= origin) & (z > 0))
        def _():
            chain_copy(buf, send, recv, origin, 1, z - 1, remote).wait_send()


def solution(mesh):
    n, n_tensor = mesh.shape["expert"], mesh.shape["tensor"]
    chips = n // 2
    grid_b = math.isqrt(chips)
    grid_a = chips // grid_b
    assert grid_a * grid_b == chips and chips == n_tensor

    def shards(picked_rows, w_gate, w_up, w_down, combine_gate, pick_owner, pick_row, residual_in, norm_gain, projection):
        _, cap, d_z = picked_rows.shape
        ff = w_gate.shape[2]
        tokens = residual_in.shape[0]
        k_dev = projection.shape[0]
        width = 384
        chunks = d_z // width
        seg = cap // n_tensor
        hbm = pl.BlockSpec(memory_space=pl.ANY)
        vmem = pl.BlockSpec(memory_space=pltpu.VMEM)
        dma = pltpu.SemaphoreType.DMA
        return pl.pallas_call(
            functools.partial(body, n, n_tensor, grid_a, grid_b, width),
            out_shape=jax.ShapeDtypeStruct((tokens, d_z), BF16),
            in_specs=[hbm, hbm, hbm, hbm, vmem, vmem, vmem, hbm, vmem, hbm],
            out_specs=vmem,
            scratch_shapes=[
                pltpu.VMEM((cap, d_z), BF16),
                pltpu.VMEM((d_z, ff), BF16),
                pltpu.VMEM((d_z, ff), BF16),
                pltpu.VMEM((ff, d_z), BF16),
                pltpu.VMEM((tokens, d_z), BF16),
                pltpu.VMEM((HALVES, cap, 2 * ff // HALVES), F32),
                pltpu.VMEM((HALVES, n_tensor, seg, 2 * ff // HALVES), BF16),
                pltpu.VMEM((HALVES, n_tensor, seg, 2 * ff // HALVES), BF16),
                pltpu.VMEM((HALVES, n_tensor, seg, ff // HALVES), BF16),
                pltpu.VMEM((chunks, chips, 2, cap, width), BF16),
                pltpu.VMEM((chunks, n_tensor, tokens, width), BF16),
                pltpu.VMEM((n * k_dev, d_z), BF16),
                pltpu.VMEM((chips, 2, tokens, cap), BF16),
                pltpu.VMEM((n_tensor, 8, tokens), F32),
                pltpu.VMEM((tokens, d_z), F32),
                dma((4 + 2 * HALVES,)),
                dma((2, HALVES, n_tensor)),
                dma((2, HALVES, n_tensor)),
                dma((HALVES, 2, n_tensor)),
                dma((HALVES, 2, n_tensor)),
                dma((chunks, chips, 2, 1)),
                dma((chunks, chips, 2)),
                dma((chunks, chips)),
                dma((chunks, chips)),
                dma((chunks, 2, n_tensor)),
                dma((chunks, 2, n_tensor)),
                dma((n_tensor,)),
                dma((n_tensor,)),
                dma((chips, 2 * PIECES)),
                dma((chips, 2 * PIECES)),
                dma((chips, 2 * PIECES)),
                dma((chips, 2 * PIECES)),
            ],
            compiler_params=pltpu.CompilerParams(
                collective_id=0, has_side_effects=True, vmem_limit_bytes=60 * 2**20
            ),
            name="layer",
        )(picked_rows, w_gate, w_up, w_down, combine_gate, pick_owner, pick_row, residual_in, norm_gain, projection)

    return jax.shard_map(
        shards,
        mesh=mesh,
        in_specs=(
            P("expert", None, "tensor"),
            P("expert", "tensor", None),
            P("expert", "tensor", None),
            P("expert", None, "tensor"),
            P("expert", None),
            P(),
            P(),
            P("expert", "tensor"),
            P("tensor"),
            P("expert", "tensor"),
        ),
        out_specs=P("expert", "tensor"),
        check_vma=False,
    )
```

```python
import functools
import math

import jax
import jax.numpy as jnp
from jax import lax
from jax.experimental import pallas as pl
from jax.experimental.pallas import tpu as pltpu
from jax.sharding import PartitionSpec as P

MESH = pl.DeviceIdType.MESH
F32 = jnp.float32
BF16 = jnp.bfloat16
HI = lax.Precision.HIGHEST
HALVES = 3
PIECES = 3


def body(
    n, n_tensor, grid_a, grid_b, width,
    rows_hbm, gate_hbm, up_hbm, down_hbm, combine_ref, owner_ref, row_ref, resid_hbm, gain_ref, proj_hbm,
    out_ref,
    x, wg, wu, wd, resid, part, from_left, from_right, hid, cbuf, ebuf, proj, table, squares, acc,
    load_sem, rs_send, rs_recv, hid_send, hid_recv, c_send, c_recv, c_sib_send, c_sib_recv,
    e_send, e_recv, s_send, s_recv, p_send, p_recv, p_sib_send, p_sib_recv,
):
    e = lax.axis_index("expert")
    z = lax.axis_index("tensor")
    core = lax.rem(e, 2)
    chip = e // 2
    a, b = chip // grid_b, lax.rem(chip, grid_b)
    last = n_tensor - 1
    cap, d_z = x.shape
    ff = wg.shape[1]
    ff_half = ff // HALVES
    seg = cap // n_tensor
    chunks = d_z // width
    tokens = resid.shape[0]
    k_dev = proj_hbm.shape[0]
    k_half = k_dev // 2
    k_piece = k_half // PIECES
    offsets = [(da, db) for da in range(grid_a) for db in range(grid_b)]

    def chip_at(da, db):
        return lax.rem(a + da + grid_a, grid_a) * grid_b + lax.rem(b + db + grid_b, grid_b)

    def to_expert(da, db):
        return {"expert": chip_at(da, db) * 2 + core}

    sibling = {"expert": chip * 2 + 1 - core}

    def remote(src, dst, send, recv, where):
        return pltpu.make_async_remote_copy(
            src_ref=src, dst_ref=dst, send_sem=send, recv_sem=recv, device_id=where, device_id_type=MESH
        )

    loads = [pltpu.make_async_copy(rows_hbm.at[0], x, load_sem.at[0])]
    for h in range(HALVES):
        cols = pl.ds(h * ff_half, ff_half)
        loads.append(pltpu.make_async_copy(gate_hbm.at[0, :, cols], wg.at[:, cols], load_sem.at[1 + 2 * h]))
        loads.append(pltpu.make_async_copy(up_hbm.at[0, :, cols], wu.at[:, cols], load_sem.at[2 + 2 * h]))
    base = 1 + 2 * HALVES
    loads.append(pltpu.make_async_copy(down_hbm.at[0], wd, load_sem.at[base]))
    loads.append(pltpu.make_async_copy(resid_hbm, resid, load_sem.at[base + 1]))
    my_k = pl.multiple_of(e * k_dev, 16)
    loads.append(pltpu.make_async_copy(proj_hbm, proj.at[pl.ds(my_k, k_dev)], load_sem.at[base + 2]))
    for load in loads:
        load.start()

    barrier = pltpu.get_barrier_semaphore()
    for i in range(1, n_tensor):
        pl.semaphore_signal(barrier, inc=1, device_id={"tensor": lax.rem(z + i, n_tensor)}, device_id_type=MESH)
    for da in range(1, grid_a):
        pl.semaphore_signal(barrier, inc=1, device_id=to_expert(da, 0), device_id_type=MESH)
    for db in range(1, grid_b):
        pl.semaphore_signal(barrier, inc=1, device_id=to_expert(0, db), device_id_type=MESH)
    pl.semaphore_signal(barrier, inc=1, device_id=sibling, device_id_type=MESH)
    pl.semaphore_wait(barrier, n_tensor - 1 + grid_a - 1 + grid_b - 1 + 1)

    sends = []

    def begin(copy):
        copy.start()
        sends.append(copy)

    def slot(da, db):
        return da * grid_b + db

    def proj_rows(da, db, k, half=None, piece=0):
        start = (chip_at(-da, -db) * 2 + k) * k_dev
        if half is None:
            return proj.at[pl.ds(pl.multiple_of(start, 16), k_dev)]
        return proj.at[pl.ds(pl.multiple_of(start + half * k_half + piece * k_piece, 16), k_piece)]

    near = [o for o in offsets[1:] if o[0] == 0 or o[1] == 0]
    far = [o for o in offsets if o[0] != 0 and o[1] != 0]

    def near_span(da, late):
        early = k_dev - k_piece
        if da != 0:
            return (early, k_piece) if late else (0, early)
        return (0, k_piece) if late else (k_piece, early)

    def near_rows(da, db, k, late):
        start, size = near_span(da, late)
        start += (chip_at(-da, -db) * 2 + k) * k_dev
        return proj.at[pl.ds(pl.multiple_of(start, 16), size)]

    def near_send(late):
        for da, db in near:
            start, size = near_span(da, late)
            s = slot(da, db)
            src = proj_hbm.at[pl.ds(start, size)]
            dst = proj.at[pl.ds(pl.multiple_of(my_k + start, 16), size)]
            begin(remote(src, dst, p_send.at[s, late], p_recv.at[s, late], to_expert(da, db)))

    mine = proj.at[pl.ds(my_k, k_dev)]
    near_send(0)
    begin(remote(proj_hbm, mine, p_sib_send.at[0, 0], p_sib_recv.at[0, 0], sibling))

    loads[0].wait()
    tile = 256
    for h in range(HALVES):
        loads[1 + 2 * h].wait()
        loads[2 + 2 * h].wait()

        @pl.loop(0, ff_half // tile)
        def _(j):
            src = pl.ds(pl.multiple_of(h * ff_half + j * tile, tile), tile)
            part[h, :, pl.ds(pl.multiple_of(j * tile, tile), tile)] = jnp.dot(
                x[...], wg[:, src], preferred_element_type=F32
            )
            part[h, :, pl.ds(pl.multiple_of(ff_half + j * tile, tile), tile)] = jnp.dot(
                x[...], wu[:, src], preferred_element_type=F32
            )

        @pl.when((z == 0) | (z == last))
        def _():
            for step in range(n_tensor - 1):
                rs_step(step, h, z, last, seg, part, from_left, from_right, rs_send, rs_recv, remote)

    def rs_middle(h):
        @pl.when((z > 0) & (z < last))
        def _():
            for step in range(n_tensor - 1):
                rs_step(step, h, z, last, seg, part, from_left, from_right, rs_send, rs_recv, remote)

    token = lax.broadcasted_iota(jnp.int32, (tokens, cap), 0)
    for da, db in offsets:
        for r in range(2):
            source = chip_at(-da, -db) * 2 + (core if r == 0 else 1 - core)
            owner = owner_ref[pl.ds(source, 1), :]
            row = row_ref[pl.ds(source, 1), :]
            target = jnp.where(owner == e, row, -1)
            table[slot(da, db), r] = jnp.where(target == token, 1.0, 0.0).astype(BF16)

    my_seg = pl.ds(pl.multiple_of(z * seg, seg), seg)
    def rs_final(h):
        @pl.when(z > 0)
        def _():
            remote(from_left.at[h, z], from_left.at[h, z], rs_send.at[0, h, z], rs_recv.at[0, h, z], {"tensor": z}).wait_recv()
            part[h, my_seg, :] += from_left[h, z].astype(F32)

        @pl.when(z < last)
        def _():
            remote(from_right.at[h, z], from_right.at[h, z], rs_send.at[1, h, z], rs_recv.at[1, h, z], {"tensor": z}).wait_recv()
            part[h, my_seg, :] += from_right[h, z].astype(F32)

        gate = part[h, my_seg, :ff_half]
        up = part[h, my_seg, ff_half:]
        hid[h, z] = (gate / (1.0 + jnp.exp(-gate)) * up).astype(BF16)
        chain_own(hid.at[h], hid_send.at[h], hid_recv.at[h], z, last, remote)

    for step in range(n_tensor + HALVES - 1):
        if step < HALVES:
            rs_middle(step)
        for h in range(HALVES):
            if 1 <= step - h < n_tensor:
                chain_pass(step - h, hid.at[h], hid_send.at[h], hid_recv.at[h], z, last, remote)
        if step < HALVES:
            rs_final(step)

    loads[base].wait()
    loads[base + 1].wait()
    weight = lax.dot_general(
        jnp.broadcast_to(combine_ref[...], (8, cap)), jnp.full((8, width), 0.125, F32),
        (((0,), (0,)), ((), ())), precision=HI, preferred_element_type=F32,
    )
    cap_half = cap // 2

    def c_block(q, da, db, r=0, half=None):
        ref = cbuf.at[q, slot(da, db), r]
        return ref if half is None else ref.at[pl.ds(half * cap_half, cap_half)]

    def stage_send(q):
        cols = pl.ds(q * width, width)
        total = 0.0
        for h in range(HALVES):
            total += jnp.dot(
                hid[h].reshape(cap, ff_half), wd[pl.ds(h * ff_half, ff_half), cols], preferred_element_type=F32
            )
        cbuf[q, 0, 0] = (weight * total).astype(BF16)
        own = c_block(q, 0, 0)
        for da, db in offsets[1:]:
            if da == 0 or db == 0:
                s = slot(da, db)
                begin(remote(own, c_block(q, da, db), c_send.at[q, s, 0, 0], c_recv.at[q, s, 0], to_expert(da, db)))
        begin(remote(own, c_block(q, 0, 0, 1), c_sib_send.at[q, 0], c_sib_recv.at[q, 0], sibling))

    def arrived(ref, send, recv):
        remote(ref, ref, send, recv, sibling).wait_recv()

    def stage_forward(q):
        for da, db in offsets[1:]:
            if da != 0 and db != 0:
                continue
            s = slot(da, db)
            block = c_block(q, da, db)
            arrived(block, c_send.at[q, s, 0, 0], c_recv.at[q, s, 0])
            if db == 0:
                for d in range(1, grid_b):
                    t = slot(da, d)
                    begin(remote(c_block(q, da, 0, 0, 0), c_block(q, da, d, 0, 0), c_send.at[q, t, 0, 0], c_recv.at[q, t, 0], to_expert(0, d)))
            else:
                for d in range(1, grid_a):
                    t = slot(d, db)
                    begin(remote(c_block(q, 0, db, 0, 1), c_block(q, d, db, 0, 1), c_send.at[q, t, 1, 0], c_recv.at[q, t, 1], to_expert(d, 0)))
            begin(remote(block, c_block(q, da, db, 1), c_sib_send.at[q, s], c_sib_recv.at[q, s], sibling))

    def stage_combine(q):
        for da, db in offsets:
            if da == 0 or db == 0:
                continue
            s = slot(da, db)
            for half in range(2):
                arrived(c_block(q, da, db, 0, half), c_send.at[q, s, half, 0], c_recv.at[q, s, half])
            block = c_block(q, da, db)
            begin(remote(block, c_block(q, da, db, 1), c_sib_send.at[q, s], c_sib_recv.at[q, s], sibling))
        cols = pl.ds(q * width, width)
        mixed = resid[:, cols].astype(F32)
        for da, db in offsets:
            s = slot(da, db)
            mixed += jnp.dot(table[s, 0], cbuf[q, s, 0], preferred_element_type=F32)
        for da, db in offsets:
            s = slot(da, db)
            arrived(c_block(q, da, db, 1), c_sib_send.at[q, s], c_sib_recv.at[q, s])
            mixed += jnp.dot(table[s, 1], cbuf[q, s, 1], preferred_element_type=F32)
        ebuf[q, z] = (mixed * gain_ref[cols].reshape(1, width)).astype(BF16)
        chain_own(ebuf.at[q], e_send.at[q], e_recv.at[q], z, last, remote)
        return lax.dot_general(
            jnp.ones((8, width), F32), mixed * mixed, (((1,), (1,)), ((), ())), precision=HI,
            preferred_element_type=F32,
        )

    square_sum = 0.0
    for t in range(chunks + 2):
        if t < chunks:
            stage_send(t)
        if 0 <= t - 1 < chunks:
            stage_forward(t - 1)
        if 0 <= t - 2 < chunks:
            square_sum += stage_combine(t - 2)
            for i in range(1, n_tensor):
                if t - 2 - i >= 0:
                    chain_pass(i, ebuf.at[t - 2 - i], e_send.at[t - 2 - i], e_recv.at[t - 2 - i], z, last, remote)
        if t == chunks:
            near_send(1)
            for da, db in near:
                block = near_rows(da, db, core, 0)
                arrived(block, p_send.at[slot(da, db), 0], p_recv.at[slot(da, db), 0])
                if db == 0:
                    for d in range(1, grid_b):
                        u = slot(da, d)
                        for piece in range(PIECES):
                            ref = proj_rows(da, 0, core, 0, piece)
                            begin(remote(ref, ref, p_send.at[u, piece], p_recv.at[u, piece], to_expert(0, d)))
                else:
                    for d in range(1, grid_a):
                        u = slot(d, db)
                        for piece in range(PIECES):
                            ref = proj_rows(0, db, core, 1, piece)
                            p = PIECES + piece
                            begin(remote(ref, ref, p_send.at[u, p], p_recv.at[u, p], to_expert(d, 0)))

    for da, db in near:
        block = near_rows(da, db, core, 0)
        begin(remote(block, block, p_sib_send.at[slot(da, db), 0], p_sib_recv.at[slot(da, db), 0], sibling))

    squares[z] = square_sum
    for i in range(1, n_tensor):
        begin(remote(squares.at[z], squares.at[z], s_send.at[i], s_recv.at[i], {"tensor": lax.rem(z + i, n_tensor)}))
    for step in range(chunks - n_tensor, chunks + n_tensor):
        for i in range(1, n_tensor):
            q = step - i
            if 0 <= q < chunks and q + i > chunks - 1:
                chain_pass(i, ebuf.at[q], e_send.at[q], e_recv.at[q], z, last, remote)

    total_squares = squares[z]
    for i in range(1, n_tensor):
        origin = lax.rem(z + n_tensor - i, n_tensor)
        remote(squares.at[origin], squares.at[origin], s_send.at[i], s_recv.at[i], {"tensor": z}).wait_recv()
        total_squares += squares[origin]
    col = 512 if d_z % 512 == 0 else 128
    column_total = lax.dot_general(
        total_squares, jnp.full((8, col), 0.125, F32), (((0,), (0,)), ((), ())), precision=HI,
        preferred_element_type=F32,
    )
    inverse_rms = lax.rsqrt(column_total / (d_z * n_tensor) + 1e-05)

    loads[base + 2].wait()
    order = [(0, 0)] + near + far

    def hand_over_late():
        for da, db in near:
            s = slot(da, db)
            block = near_rows(da, db, core, 1)
            arrived(block, p_send.at[s, 1], p_recv.at[s, 1])
            begin(remote(block, block, p_sib_send.at[s, 1], p_sib_recv.at[s, 1], sibling))

    def hand_over(piece):
        for da, db in far:
            s = slot(da, db)
            for half in range(2):
                p = half * PIECES + piece
                block = proj_rows(da, db, core, half, piece)
                arrived(block, p_send.at[s, p], p_recv.at[s, p])
                begin(remote(block, block, p_sib_send.at[s, p], p_sib_recv.at[s, p], sibling))

    assert len(near) + 1 >= PIECES
    for pos, (da, db) in enumerate(order):
        s = slot(da, db)
        if pos == 0:
            arrived(proj_rows(da, db, 1 - core), p_sib_send.at[s, 0], p_sib_recv.at[s, 0])
        elif pos <= len(near):
            for late in range(2):
                arrived(near_rows(da, db, 1 - core, late), p_sib_send.at[s, late], p_sib_recv.at[s, late])
        else:
            for half in range(2):
                for piece in range(PIECES):
                    p = half * PIECES + piece
                    arrived(proj_rows(da, db, 1 - core, half, piece), p_sib_send.at[s, p], p_sib_recv.at[s, p])
        source = chip_at(-da, -db)

        @pl.loop(0, d_z // col)
        def _(j):
            cols = pl.ds(pl.multiple_of(j * col, col), col)
            total = 0.0 if pos == 0 else acc[:, cols]
            for q in range(chunks):
                k = pl.ds(pl.multiple_of(source * 2 * k_dev + q * width, 128), width)
                total += jnp.dot(ebuf[q, source], proj[k, cols], preferred_element_type=F32)
            if pos == len(order) - 1:
                out_ref[:, cols] = (total * inverse_rms).astype(BF16)
            else:
                acc[:, cols] = total

        if pos == 0:
            hand_over_late()
        if pos < PIECES:
            hand_over(pos)

    for copy in sends:
        copy.wait_send()
    for h in range(HALVES):
        for step in range(n_tensor - 1):
            right, left = n_tensor - 1 - step, step

            @pl.when(z < right)
            def _():
                remote(from_left.at[h, right], from_left.at[h, right], rs_send.at[0, h, right], rs_recv.at[0, h, right], {"tensor": z + 1}).wait_send()

            @pl.when(z > left)
            def _():
                remote(from_right.at[h, left], from_right.at[h, left], rs_send.at[1, h, left], rs_recv.at[1, h, left], {"tensor": z - 1}).wait_send()
        chain_end(hid.at[h], hid_send.at[h], hid_recv.at[h], z, last, remote)
    for q in range(chunks):
        chain_end(ebuf.at[q], e_send.at[q], e_recv.at[q], z, last, remote)


def rs_step(step, h, z, last, seg, part, from_left, from_right, send, recv, remote):
    right, left = last - step, step

    def go_right():
        @pl.when(z < right)
        def _():
            block = part[h, pl.ds(right * seg, seg), :]
            slot = from_left.at[h, right]
            copy = remote(slot, slot, send.at[0, h, right], recv.at[0, h, right], {"tensor": z + 1})

            @pl.when(z > 0)
            def _():
                copy.wait_recv()
                from_left[h, right] = (from_left[h, right].astype(F32) + block).astype(BF16)

            @pl.when(z == 0)
            def _():
                from_left[h, right] = block.astype(BF16)

            copy.start()

    def go_left():
        @pl.when(z > left)
        def _():
            block = part[h, pl.ds(left * seg, seg), :]
            slot = from_right.at[h, left]
            copy = remote(slot, slot, send.at[1, h, left], recv.at[1, h, left], {"tensor": z - 1})

            @pl.when(z < last)
            def _():
                copy.wait_recv()
                from_right[h, left] = (from_right[h, left].astype(F32) + block).astype(BF16)

            @pl.when(z == last)
            def _():
                from_right[h, left] = block.astype(BF16)

            copy.start()

    @pl.when(2 * z < last)
    def _():
        go_right()
        go_left()

    @pl.when(2 * z >= last)
    def _():
        go_left()
        go_right()


def chain_copy(buf, send, recv, origin, way, target, remote):
    return remote(buf.at[origin], buf.at[origin], send.at[way, origin], recv.at[way, origin], {"tensor": target})


def chain_own(buf, send, recv, z, last, remote):
    @pl.when(z < last)
    def _():
        chain_copy(buf, send, recv, z, 0, z + 1, remote).start()

    @pl.when(z > 0)
    def _():
        chain_copy(buf, send, recv, z, 1, z - 1, remote).start()


def chain_pass(i, buf, send, recv, z, last, remote):
    @pl.when(z >= i)
    def _():
        copy = chain_copy(buf, send, recv, z - i, 0, z + 1, remote)
        copy.wait_recv()

        @pl.when(z < last)
        def _():
            copy.start()

    @pl.when(z + i <= last)
    def _():
        copy = chain_copy(buf, send, recv, z + i, 1, z - 1, remote)
        copy.wait_recv()

        @pl.when(z > 0)
        def _():
            copy.start()


def chain_end(buf, send, recv, z, last, remote):
    for origin in range(last + 1):
        @pl.when((z >= origin) & (z < last))
        def _():
            chain_copy(buf, send, recv, origin, 0, z + 1, remote).wait_send()

        @pl.when((z <= origin) & (z > 0))
        def _():
            chain_copy(buf, send, recv, origin, 1, z - 1, remote).wait_send()


def solution(mesh):
    n, n_tensor = mesh.shape["expert"], mesh.shape["tensor"]
    chips = n // 2
    grid_b = math.isqrt(chips)
    grid_a = chips // grid_b
    assert grid_a * grid_b == chips and chips == n_tensor

    def shards(picked_rows, w_gate, w_up, w_down, combine_gate, pick_owner, pick_row, residual_in, norm_gain, projection):
        _, cap, d_z = picked_rows.shape
        ff = w_gate.shape[2]
        tokens = residual_in.shape[0]
        k_dev = projection.shape[0]
        width = 384
        chunks = d_z // width
        seg = cap // n_tensor
        hbm = pl.BlockSpec(memory_space=pl.ANY)
        vmem = pl.BlockSpec(memory_space=pltpu.VMEM)
        dma = pltpu.SemaphoreType.DMA
        return pl.pallas_call(
            functools.partial(body, n, n_tensor, grid_a, grid_b, width),
            out_shape=jax.ShapeDtypeStruct((tokens, d_z), BF16),
            in_specs=[hbm, hbm, hbm, hbm, vmem, vmem, vmem, hbm, vmem, hbm],
            out_specs=vmem,
            scratch_shapes=[
                pltpu.VMEM((cap, d_z), BF16),
                pltpu.VMEM((d_z, ff), BF16),
                pltpu.VMEM((d_z, ff), BF16),
                pltpu.VMEM((ff, d_z), BF16),
                pltpu.VMEM((tokens, d_z), BF16),
                pltpu.VMEM((HALVES, cap, 2 * ff // HALVES), F32),
                pltpu.VMEM((HALVES, n_tensor, seg, 2 * ff // HALVES), BF16),
                pltpu.VMEM((HALVES, n_tensor, seg, 2 * ff // HALVES), BF16),
                pltpu.VMEM((HALVES, n_tensor, seg, ff // HALVES), BF16),
                pltpu.VMEM((chunks, chips, 2, cap, width), BF16),
                pltpu.VMEM((chunks, n_tensor, tokens, width), BF16),
                pltpu.VMEM((n * k_dev, d_z), BF16),
                pltpu.VMEM((chips, 2, tokens, cap), BF16),
                pltpu.VMEM((n_tensor, 8, tokens), F32),
                pltpu.VMEM((tokens, d_z), F32),
                dma((4 + 2 * HALVES,)),
                dma((2, HALVES, n_tensor)),
                dma((2, HALVES, n_tensor)),
                dma((HALVES, 2, n_tensor)),
                dma((HALVES, 2, n_tensor)),
                dma((chunks, chips, 2, 1)),
                dma((chunks, chips, 2)),
                dma((chunks, chips)),
                dma((chunks, chips)),
                dma((chunks, 2, n_tensor)),
                dma((chunks, 2, n_tensor)),
                dma((n_tensor,)),
                dma((n_tensor,)),
                dma((chips, 2 * PIECES)),
                dma((chips, 2 * PIECES)),
                dma((chips, 2 * PIECES)),
                dma((chips, 2 * PIECES)),
            ],
            compiler_params=pltpu.CompilerParams(
                collective_id=0, has_side_effects=True, vmem_limit_bytes=60 * 2**20
            ),
            name="layer",
        )(picked_rows, w_gate, w_up, w_down, combine_gate, pick_owner, pick_row, residual_in, norm_gain, projection)

    return jax.shard_map(
        shards,
        mesh=mesh,
        in_specs=(
            P("expert", None, "tensor"),
            P("expert", "tensor", None),
            P("expert", "tensor", None),
            P("expert", None, "tensor"),
            P("expert", None),
            P(),
            P(),
            P("expert", "tensor"),
            P("tensor"),
            P("expert", "tensor"),
        ),
        out_specs=P("expert", "tensor"),
        check_vma=False,
    )
```
